256 devices in a mesh: rows: 64 (over z, x, core), bal: 4 (over y).
Axes of the slice: x: 4, y: 4, z: 8, core: 2. Of those that a mesh axis runs over, the one named last changes fastest.
Arguments:
- embeddings: bfloat16 [131072, 1024], P(('rows', 'bal')), may hold values from -60 to 60
- cluster_blocks: int32 [128], replicated, may hold values from 1 to 4, as said below
Outputs:
- row_max: float32 [131072], P(('rows', 'bal'))
The draws below stay inside these ranges and needn't reach their ends.
Inputs may be any that keep to these rules, and one draw needn't show every extreme that they name: `cluster_blocks`: the sizes sum to 256; at least one cluster has exactly 4 blocks.
All inputs are finite; a program needn't handle non-finite values.
Results may differ from the reference program's by a relative error of at most 0.00051.
Values may be sent and summed in bfloat16 or wider, within the bound.
No kernel may reach another device: no remote copies, remote signals or barrier semaphores. Data moves between devices by JAX's collectives and lax.ppermute only.
A program may use at most 64 MiB of HBM per device.

```python
import jax
import jax.numpy as jnp
from jax import lax

D = 1024
BLOCK = 512
MAXB = 4
NBLK = 256
NCL = 128


def fill_segment(sizes, key, first, last, extra):
    slots = jnp.arange(NCL, dtype=jnp.int32)
    picks = jax.random.randint(jax.random.fold_in(key, 22), (extra,), 0, NCL)
    shuffled = jax.random.permutation(jax.random.fold_in(key, 23), NCL).astype(jnp.int32)
    outside = ((slots < first) | (slots >= last)).astype(jnp.int32)

    def place(counts, pick):
        biased = shuffled[pick * pick // NCL]
        distance = (slots - biased) % NCL
        blocked = jnp.maximum((counts >= MAXB).astype(jnp.int32), outside)
        target = jnp.argmin(distance + NCL * blocked)
        return (counts.at[target].add(1), 0)
    sizes, _ = lax.scan(place, sizes, picks)
    return sizes


def cluster_sizes(key):
    special = NCL // 2
    sizes = jnp.ones((NCL,), jnp.int32).at[special].set(MAXB)
    front_extra = NBLK // 2 - 2 - special
    back_extra = NBLK - NBLK // 2 - 2 - (NCL - special - 1)
    sizes = fill_segment(sizes, jax.random.fold_in(key, 41), 0, special, front_extra)
    sizes = fill_segment(sizes, jax.random.fold_in(key, 42), special + 1, NCL, back_extra)
    return sizes


def draw_cluster_blocks(key, part):
    return cluster_sizes(jax.random.fold_in(key, 7))


def draw_embeddings(key, part):
    sizes = cluster_sizes(jax.random.fold_in(key, 7))
    bounds = jnp.cumsum(sizes)
    starts = bounds - sizes
    blocks_all = jnp.arange(NBLK, dtype=jnp.int32)
    owner = jnp.sum((bounds[None, :] <= blocks_all[:, None]).astype(jnp.int32), axis=1)
    first_block = starts[owner]
    span_blocks = sizes[owner]
    total_rows = NBLK * BLOCK
    row_block = jnp.arange(total_rows, dtype=jnp.int32) // BLOCK
    jumps = jax.random.randint(jax.random.fold_in(key, 31), (total_rows,), 0, MAXB * BLOCK)
    partner_block = first_block[row_block] + jumps // BLOCK % span_blocks[row_block]
    partner_row = partner_block * BLOCK + jumps % BLOCK
    weight_dup = jax.random.uniform(jax.random.fold_in(key, 33), (total_rows, 1), jnp.float32, 0.3, 2.0)
    base = jnp.clip(jax.random.normal(jax.random.fold_in(key, 32), (total_rows, D), jnp.float32), -6.0, 6.0)
    mixed = base + weight_dup * base[partner_row]
    return mixed.astype(jnp.bfloat16)


def setup_inputs(seed: int = 0) -> dict:
    key_list = jax.random.split(jax.random.key(seed), 3)
    embeddings = draw_embeddings(jax.random.fold_in(key_list[2], 71), 0)
    cluster_blocks = draw_cluster_blocks(jax.random.fold_in(key_list[2], 71), 0)
    return {"embeddings": embeddings, "cluster_blocks": cluster_blocks}


EPSILON = 1e-06

def unit_rows(block_rows):
    values = block_rows.astype(jnp.float32)
    scaled = values * lax.rsqrt(lax.optimization_barrier(jnp.sum(values * values, axis=1, keepdims=True)) + EPSILON)
    return scaled.astype(jnp.bfloat16)

def reference(embeddings, cluster_blocks):
    blocks_all = embeddings.shape[0] // BLOCK
    normed = unit_rows(embeddings).astype(jnp.float32).reshape(blocks_all, BLOCK, D)
    bounds = jnp.cumsum(cluster_blocks).astype(jnp.int32)
    positions = jnp.arange(blocks_all, dtype=jnp.int32)
    diagonal_mask = jnp.arange(BLOCK)[:, None] == jnp.arange(BLOCK)[None, :]
    highest = jnp.full((blocks_all, BLOCK), -2.0, jnp.float32)
    for offset in range(MAXB):
        if offset == 0:
            partner = normed
        else:
            partner = jnp.concatenate([jnp.zeros((offset, BLOCK, D), jnp.float32), normed[:-offset]], axis=0)
        lower = positions - offset
        crossing = lax.optimization_barrier(jnp.sum(((bounds[None, :] > lower[:, None]) & (bounds[None, :] <= positions[:, None])).astype(jnp.int32), axis=1))
        allowed = (lower >= 0) & (crossing == 0)

        def tile(items):
            mine, theirs, permitted = items
            products = jnp.dot(mine, theirs.T, precision=lax.Precision.HIGHEST)
            products = jnp.where(permitted, products, -2.0)
            if offset == 0:
                products = jnp.where(diagonal_mask, -2.0, products)
            return (lax.optimization_barrier(jnp.max(products, axis=1)), lax.optimization_barrier(jnp.max(products, axis=0)))
        row_part, col_part = lax.map(tile, (normed, partner, allowed))
        highest = jnp.maximum(highest, row_part)
        if offset > 0:
            returned = jnp.concatenate([col_part[offset:], jnp.full((offset, BLOCK), -2.0, jnp.float32)], axis=0)
            highest = jnp.maximum(highest, returned)
    return highest.reshape(-1)
```

```python
import jax
import jax.numpy as jnp
from jax import lax
from jax.experimental import pallas as pl
from jax.experimental.pallas import tpu as pltpu
from jax.sharding import PartitionSpec as P

EPSILON = 1e-06
AXES = ("rows", "bal")
LOWEST = -2.0
STRIP = 64


def shifted(block, distance):
    n = lax.axis_size(AXES)
    return lax.ppermute(block, AXES, [(i, (i + distance) % n) for i in range(n)])


def joined(bounds, lower, distance):
    n = lax.axis_size(AXES)
    lower = lax.rem(lower + n, n)
    upper = lower + distance
    crossing = jnp.sum(((bounds > lower) & (bounds <= upper)).astype(jnp.int32))
    return ((upper < n) & (crossing == 0)).astype(jnp.int32)


def write_units(raw_ref, unit_ref):
    for start in range(0, raw_ref.shape[0], STRIP):
        rows = pl.ds(start, STRIP)
        values = raw_ref[rows, :].astype(jnp.float32)
        scale = lax.rsqrt(jnp.sum(values * values, axis=1, keepdims=True) + EPSILON)
        unit_ref[rows, :] = (values * scale).astype(jnp.bfloat16)


def products_of(left, right):
    return lax.dot_general(
        left, right, (((1,), (1,)), ((), ())), preferred_element_type=jnp.float32
    )


def column_max(products):
    return jnp.max(products, axis=0, keepdims=True)


def row_max(products):
    width = products.shape[1]
    folded = products[:, :128]
    for start in range(128, width, 128):
        folded = jnp.maximum(folded, products[:, start : start + 128])
    return jnp.max(folded.T, axis=0, keepdims=True)


def own_kernel(raw_ref, unit_ref, high_ref):
    write_units(raw_ref, unit_ref)
    products = products_of(unit_ref[...], unit_ref[...])
    row = lax.broadcasted_iota(jnp.int32, products.shape, 0)
    col = lax.broadcasted_iota(jnp.int32, products.shape, 1)
    high_ref[...] = column_max(jnp.where(row == col, LOWEST, products))


def far_kernel(down_ref, up_ref, down_unit_ref, up_unit_ref):
    write_units(down_ref, down_unit_ref)
    write_units(up_ref, up_unit_ref)


def prev_kernel(flags_ref, raw_ref, own_ref, far_ref, high_in_ref, unit_ref, high_ref, back_ref):
    write_units(raw_ref, unit_ref)
    high_ref[...] = high_in_ref[...]
    back_ref[...] = jnp.full_like(back_ref, LOWEST)

    @pl.when(flags_ref[0] == 1)
    def _():
        products = products_of(own_ref[...], unit_ref[...])
        high_ref[...] = jnp.maximum(high_ref[...], row_max(products))
        back_ref[...] = column_max(products)

    @pl.when(flags_ref[2] == 1)
    def _():
        back_ref[...] = jnp.maximum(
            back_ref[...], column_max(products_of(far_ref[...], unit_ref[...]))
        )


def next_kernel(flags_ref, raw_ref, prev_ref, far_ref, back_in_ref, back_ref, ahead_ref, unit_ref):
    back_ref[...] = back_in_ref[...]
    ahead_ref[...] = jnp.full_like(ahead_ref, LOWEST)

    @pl.when(flags_ref[1] + flags_ref[3] > 0)
    def _():
        write_units(raw_ref, unit_ref)

    @pl.when(flags_ref[1] == 1)
    def _():
        products = products_of(prev_ref[...], unit_ref[...])
        back_ref[...] = jnp.maximum(back_ref[...], row_max(products))
        ahead_ref[...] = column_max(products)

    @pl.when(flags_ref[3] == 1)
    def _():
        ahead_ref[...] = jnp.maximum(
            ahead_ref[...], column_max(products_of(far_ref[...], unit_ref[...]))
        )


VMEM = pl.BlockSpec(memory_space=pltpu.VMEM)
SMEM = pl.BlockSpec(memory_space=pltpu.SMEM)
PARAMS = pltpu.CompilerParams(vmem_limit_bytes=40 * 1024 * 1024)


def call(kernel, args, outs, scratch=(), flops=0):
    specs = [SMEM if a.ndim == 1 else VMEM for a in args]
    moved = sum(a.size * a.dtype.itemsize for a in args)
    return pl.pallas_call(
        kernel,
        in_specs=specs,
        out_specs=[VMEM] * len(outs),
        out_shape=[jax.ShapeDtypeStruct(*o) for o in outs],
        scratch_shapes=list(scratch),
        compiler_params=PARAMS,
        cost_estimate=pl.CostEstimate(flops=flops, bytes_accessed=moved, transcendentals=0),
    )(*args)


def shards(embeddings, cluster_blocks):
    block, width = embeddings.shape
    from_prev = shifted(embeddings, 1)
    from_next = shifted(embeddings, -1)
    from_down = shifted(embeddings, 4)
    from_up = shifted(embeddings, -4)

    bounds = jnp.cumsum(cluster_blocks)
    me = lax.axis_index(AXES)
    flags = jnp.stack(
        [
            joined(bounds, me - 1, 1),
            joined(bounds, me - 1, 2),
            joined(bounds, me - 4, 3),
            joined(bounds, me + 1, 3),
        ]
    )
    units = ((block, width), jnp.bfloat16)
    line = ((1, block), jnp.float32)
    tile = 2 * block * block * width

    own, high = call(own_kernel, (embeddings,), [units, line], flops=tile)
    down, up = call(far_kernel, (from_down, from_up), [units, units])
    prev, high, back = call(
        prev_kernel, (flags, from_prev, own, down, high), [units, line, line], flops=2 * tile
    )
    back, ahead = call(
        next_kernel,
        (flags, from_next, prev, up, back),
        [line, line],
        scratch=[pltpu.VMEM(*units)],
        flops=2 * tile,
    )
    returned = jnp.maximum(shifted(back, -1), shifted(ahead, 1))
    return jnp.maximum(high, returned).reshape(block)


def solution(mesh):
    in_specs = (P(AXES, None), P())
    out_specs = P(AXES)
    return jax.shard_map(shards, mesh=mesh, in_specs=in_specs, out_specs=out_specs, check_vma=False)
```

```python
import jax
import jax.numpy as jnp
from jax import lax
from jax.experimental import pallas as pl
from jax.experimental.pallas import tpu as pltpu
from jax.sharding import PartitionSpec as P

EPSILON = 1e-06
AXES = ("rows", "bal")
LOWEST = -2.0
STRIP = 64


def pair_mate(i, n):
    return i ^ 1


def other_neighbour(i, n):
    return (i + 1) % n if i % 2 else (i - 1) % n


def core_mate(i, n):
    return i ^ 4


def column_neighbour(i, n):
    return (i + 4) % n if i // 4 % 2 else (i - 4) % n


def swapped(block, partner):
    n = lax.axis_size(AXES)
    return lax.ppermute(block, AXES, [(i, partner(i, n)) for i in range(n)])


def joined(bounds, lower, distance):
    n = lax.axis_size(AXES)
    lower = lax.rem(lower + n, n)
    upper = lower + distance
    crossing = jnp.sum(((bounds > lower) & (bounds <= upper)).astype(jnp.int32))
    return ((upper < n) & (crossing == 0)).astype(jnp.int32)


def write_units(raw_ref, unit_ref):
    for start in range(0, raw_ref.shape[0], STRIP):
        rows = pl.ds(start, STRIP)
        values = raw_ref[rows, :].astype(jnp.float32)
        scale = lax.rsqrt(jnp.sum(values * values, axis=1, keepdims=True) + EPSILON)
        unit_ref[rows, :] = (values * scale).astype(jnp.bfloat16)


def products_of(left, right):
    return lax.dot_general(
        left, right, (((1,), (1,)), ((), ())), preferred_element_type=jnp.float32
    )


def column_max(products):
    return jnp.max(products, axis=0, keepdims=True)


def row_max(products):
    width = products.shape[1]
    folded = products[:, :128]
    for start in range(128, width, 128):
        folded = jnp.maximum(folded, products[:, start : start + 128])
    return jnp.max(folded.T, axis=0, keepdims=True)


def own_kernel(raw_ref, unit_ref, high_ref):
    write_units(raw_ref, unit_ref)
    products = products_of(unit_ref[...], unit_ref[...])
    row = lax.broadcasted_iota(jnp.int32, products.shape, 0)
    col = lax.broadcasted_iota(jnp.int32, products.shape, 1)
    high_ref[...] = column_max(jnp.where(row == col, LOWEST, products))


def other_kernel(flags_ref, raw_ref, own_ref, high_in_ref, unit_ref, high_ref):
    write_units(raw_ref, unit_ref)
    high_ref[...] = high_in_ref[...]

    @pl.when(flags_ref[0] == 1)
    def _():
        products = products_of(unit_ref[...], own_ref[...])
        high_ref[...] = jnp.maximum(high_ref[...], column_max(products))


def mate_kernel(
    flags_ref, raw_ref, own_ref, other_ref, core_ref, column_ref, high_in_ref,
    high_ref, back_ref, unit_ref,
):
    write_units(raw_ref, unit_ref)
    high_ref[...] = high_in_ref[...]
    back_ref[...] = jnp.full_like(back_ref, LOWEST)

    @pl.when(flags_ref[1] == 1)
    def _():
        products = products_of(unit_ref[...], own_ref[...])
        high_ref[...] = jnp.maximum(high_ref[...], column_max(products))

    @pl.when(flags_ref[2] == 1)
    def _():
        products = products_of(other_ref[...], unit_ref[...])
        back_ref[0] = row_max(products)
        back_ref[1] = column_max(products)

    for slot, far_ref in ((3, core_ref), (5, column_ref)):

        @pl.when((flags_ref[slot] == 1) & (flags_ref[slot + 1] == 0))
        def _():
            products = products_of(far_ref[...], other_ref[...])
            back_ref[0] = jnp.maximum(back_ref[0], column_max(products))

        @pl.when((flags_ref[slot] == 1) & (flags_ref[slot + 1] == 1))
        def _():
            products = products_of(far_ref[...], unit_ref[...])
            back_ref[1] = jnp.maximum(back_ref[1], column_max(products))


VMEM = pl.BlockSpec(memory_space=pltpu.VMEM)
SMEM = pl.BlockSpec(memory_space=pltpu.SMEM)
PARAMS = pltpu.CompilerParams(vmem_limit_bytes=40 * 1024 * 1024)


def call(kernel, args, outs, scratch=(), flops=0):
    specs = [SMEM if a.ndim == 1 else VMEM for a in args]
    moved = sum(a.size * a.dtype.itemsize for a in args)
    return pl.pallas_call(
        kernel,
        in_specs=specs,
        out_specs=[VMEM] * len(outs),
        out_shape=[jax.ShapeDtypeStruct(*o) for o in outs],
        scratch_shapes=list(scratch),
        compiler_params=PARAMS,
        cost_estimate=pl.CostEstimate(flops=flops, bytes_accessed=moved, transcendentals=0),
    )(*args)


def shards(embeddings, cluster_blocks):
    block, width = embeddings.shape
    from_other = swapped(embeddings, other_neighbour)
    from_mate = swapped(embeddings, pair_mate)

    bounds = jnp.cumsum(cluster_blocks)
    me = lax.axis_index(AXES)
    odd = me % 2
    second = me // 4 % 2
    with_prev = joined(bounds, me - 1, 1)
    with_next = joined(bounds, me, 1)
    around = joined(bounds, me - 1, 2)
    before = joined(bounds, me - 4, 3)
    after = joined(bounds, me + 1, 3)
    flags = jnp.stack(
        [
            jnp.where(odd == 1, with_next, with_prev),
            jnp.where(odd == 1, with_prev, with_next),
            around,
            jnp.where(second == 1, before, after),
            jnp.where(second == 1, odd, 1 - odd),
            jnp.where(second == 1, after, before),
            jnp.where(second == 1, 1 - odd, odd),
        ]
    )
    units = ((block, width), jnp.bfloat16)
    line = ((1, block), jnp.float32)
    tile = 2 * block * block * width

    own, high = call(own_kernel, (embeddings,), [units, line], flops=tile)
    column = swapped(own, column_neighbour)
    core = swapped(own, core_mate)
    other, high = call(other_kernel, (flags, from_other, own, high), [units, line], flops=tile)
    high, back = call(
        mate_kernel,
        (flags, from_mate, own, other, core, column, high),
        [line, ((2, 1, block), jnp.float32)],
        scratch=[pltpu.VMEM(*units)],
        flops=2 * tile,
    )
    returned = jnp.maximum(swapped(back[0], other_neighbour), swapped(back[1], pair_mate))
    return jnp.maximum(high, returned).reshape(block)


def solution(mesh):
    in_specs = (P(AXES, None), P())
    out_specs = P(AXES)
    return jax.shard_map(shards, mesh=mesh, in_specs=in_specs, out_specs=out_specs, check_vma=False)
```

```python
import jax
import jax.numpy as jnp
from jax import lax
from jax.experimental import pallas as pl
from jax.experimental.pallas import tpu as pltpu
from jax.sharding import PartitionSpec as P

EPSILON = 1e-06
AXES = ("rows", "bal")
LOWEST = -2.0
STRIP = 64


def pair_mate(i, n):
    return i ^ 1


def other_neighbour(i, n):
    j = i + 1 if i % 2 else i - 1
    return j if 0 <= j < n else None


def core_mate(i, n):
    return i ^ 4


def column_neighbour(i, n):
    j = i + 4 if i // 4 % 2 else i - 4
    return j if 0 <= j < n else i ^ 3


def swapped(block, partner):
    n = lax.axis_size(AXES)
    pairs = [(i, partner(i, n)) for i in range(n)]
    return lax.ppermute(block, AXES, [p for p in pairs if p[1] is not None])


def joined(bounds, lower, distance):
    upper = lower + distance
    crossing = jnp.sum(((bounds > lower) & (bounds <= upper)).astype(jnp.int32))
    inside = (lower >= 0) & (upper < lax.axis_size(AXES))
    return (inside & (crossing == 0)).astype(jnp.int32)


def write_units(raw_ref, unit_ref):
    for start in range(0, raw_ref.shape[0], STRIP):
        rows = pl.ds(start, STRIP)
        values = raw_ref[rows, :].astype(jnp.float32)
        scale = lax.rsqrt(jnp.sum(values * values, axis=1, keepdims=True) + EPSILON)
        unit_ref[rows, :] = (values * scale).astype(jnp.bfloat16)


def products_of(left, right):
    return lax.dot_general(
        left, right, (((1,), (1,)), ((), ())), preferred_element_type=jnp.float32
    )


def column_max(products):
    return jnp.max(products, axis=0, keepdims=True)


def row_max(products):
    width = products.shape[1]
    folded = products[:, :128]
    for start in range(128, width, 128):
        folded = jnp.maximum(folded, products[:, start : start + 128])
    return jnp.max(folded.T, axis=0, keepdims=True)


def own_kernel(raw_ref, unit_ref, high_ref):
    write_units(raw_ref, unit_ref)
    products = products_of(unit_ref[...], unit_ref[...])
    row = lax.broadcasted_iota(jnp.int32, products.shape, 0)
    col = lax.broadcasted_iota(jnp.int32, products.shape, 1)
    high_ref[...] = column_max(jnp.where(row == col, LOWEST, products))


def other_kernel(flags_ref, raw_ref, own_ref, high_in_ref, unit_ref, high_ref):
    write_units(raw_ref, unit_ref)
    high_ref[...] = high_in_ref[...]

    @pl.when(flags_ref[0] == 1)
    def _():
        products = products_of(unit_ref[...], own_ref[...])
        high_ref[...] = jnp.maximum(high_ref[...], column_max(products))


def mate_kernel(flags_ref, raw_ref, other_ref, unit_ref, to_other_ref, to_mate_ref):
    write_units(raw_ref, unit_ref)
    to_other_ref[...] = jnp.full_like(to_other_ref, LOWEST)
    to_mate_ref[...] = jnp.full_like(to_mate_ref, LOWEST)

    @pl.when(flags_ref[2] == 1)
    def _():
        products = products_of(other_ref[...], unit_ref[...])
        to_other_ref[...] = row_max(products)
        to_mate_ref[...] = column_max(products)


def far_kernel(
    flags_ref, core_ref, column_ref, other_ref, mate_ref, own_ref, other_in_ref, mate_in_ref, high_in_ref,
    to_other_ref, to_mate_ref, high_ref,
):
    to_other_ref[...] = other_in_ref[...]
    to_mate_ref[...] = mate_in_ref[...]
    high_ref[...] = high_in_ref[...]
    for far_ref, slot, near_ref, line_ref in (
        (core_ref, 3, other_ref, to_other_ref),
        (core_ref, 4, mate_ref, to_mate_ref),
        (column_ref, 5, other_ref, to_other_ref),
        (column_ref, 6, mate_ref, to_mate_ref),
        (column_ref, 7, own_ref, high_ref),
    ):

        @pl.when(flags_ref[slot] == 1)
        def _():
            products = products_of(far_ref[...], near_ref[...])
            line_ref[...] = jnp.maximum(line_ref[...], column_max(products))


def last_kernel(flags_ref, mate_ref, own_ref, high_in_ref, high_ref):
    high_ref[...] = high_in_ref[...]

    @pl.when(flags_ref[1] == 1)
    def _():
        products = products_of(mate_ref[...], own_ref[...])
        high_ref[...] = jnp.maximum(high_ref[...], column_max(products))


VMEM = pl.BlockSpec(memory_space=pltpu.VMEM)
SMEM = pl.BlockSpec(memory_space=pltpu.SMEM)
PARAMS = pltpu.CompilerParams(vmem_limit_bytes=40 * 1024 * 1024)


def call(kernel, args, outs, scratch=(), flops=0):
    specs = [SMEM if a.ndim == 1 else VMEM for a in args]
    moved = sum(a.size * a.dtype.itemsize for a in args)
    return pl.pallas_call(
        kernel,
        in_specs=specs,
        out_specs=[VMEM] * len(outs),
        out_shape=[jax.ShapeDtypeStruct(*o) for o in outs],
        scratch_shapes=list(scratch),
        compiler_params=PARAMS,
        cost_estimate=pl.CostEstimate(flops=flops, bytes_accessed=moved, transcendentals=0),
    )(*args)


def shards(embeddings, cluster_blocks):
    block, width = embeddings.shape
    from_other = swapped(embeddings, other_neighbour)
    from_mate = swapped(embeddings, pair_mate)

    bounds = jnp.cumsum(cluster_blocks)
    me = lax.axis_index(AXES)
    odd = me % 2
    second = me // 4 % 2
    with_prev = joined(bounds, me - 1, 1)
    with_next = joined(bounds, me, 1)
    around = joined(bounds, me - 1, 2)
    before = joined(bounds, me - 4, 3)
    after = joined(bounds, me + 1, 3)
    edge = jnp.where(me == 0, joined(bounds, 0, 3), 0)
    last = lax.axis_size(AXES) - 1
    edge = jnp.where(me == last, joined(bounds, last - 3, 3), edge)
    with_core = jnp.where(second == 1, before, after)
    with_column = jnp.where(second == 1, after, before)
    core_to_mate = jnp.where(second == 1, odd, 1 - odd)
    flags = jnp.stack(
        [
            jnp.where(odd == 1, with_next, with_prev),
            jnp.where(odd == 1, with_prev, with_next),
            around,
            with_core * (1 - core_to_mate),
            with_core * core_to_mate,
            with_column * core_to_mate,
            with_column * (1 - core_to_mate),
            edge,
        ]
    )
    units = ((block, width), jnp.bfloat16)
    line = ((1, block), jnp.float32)
    tile = 2 * block * block * width

    own, high = call(own_kernel, (embeddings,), [units, line], flops=tile)
    column = swapped(own, column_neighbour)
    core = swapped(own, core_mate)
    other, high = call(other_kernel, (flags, from_other, own, high), [units, line], flops=tile)
    mate, to_other, to_mate = call(
        mate_kernel, (flags, from_mate, other), [units, line, line], flops=tile
    )
    to_other, to_mate, high = call(
        far_kernel,
        (flags, core, column, other, mate, own, to_other, to_mate, high),
        [line, line, line],
        flops=tile,
    )
    returned = swapped(to_other, other_neighbour), swapped(to_mate, pair_mate)
    high = call(last_kernel, (flags, mate, own, high), [line], flops=tile)[0]
    has_other = (me > 0) & (me < last)
    returned = jnp.maximum(jnp.where(has_other, returned[0], LOWEST), returned[1])
    return jnp.maximum(high, returned).reshape(block)


def solution(mesh):
    in_specs = (P(AXES, None), P())
    out_specs = P(AXES)
    return jax.shard_map(shards, mesh=mesh, in_specs=in_specs, out_specs=out_specs, check_vma=False)
```

```python
import jax
import jax.numpy as jnp
from jax import lax
from jax.experimental import pallas as pl
from jax.experimental.pallas import tpu as pltpu
from jax.sharding import PartitionSpec as P

EPSILON = 1e-06
AXES = ("rows", "bal")
LOWEST = -2.0
STRIP = 64


def pair_mate(i, n):
    return i ^ 1


def other_neighbour(i, n):
    j = i + 1 if i % 2 else i - 1
    return j if 0 <= j < n else None


def core_mate(i, n):
    return i ^ 4


def column_neighbour(i, n):
    j = i + 4 if i // 4 % 2 else i - 4
    return j if 0 <= j < n else None


def to_the_ends(i, n):
    return {4: 0, n - 5: n - 1}.get(i)


def swapped(block, partner):
    n = lax.axis_size(AXES)
    pairs = [(i, partner(i, n)) for i in range(n)]
    return lax.ppermute(block, AXES, [p for p in pairs if p[1] is not None])


def joined(bounds, lower, distance):
    upper = lower + distance
    crossing = jnp.sum(((bounds > lower) & (bounds <= upper)).astype(jnp.int32))
    inside = (lower >= 0) & (upper < lax.axis_size(AXES))
    return (inside & (crossing == 0)).astype(jnp.int32)


def write_units(raw_ref, unit_ref):
    for start in range(0, raw_ref.shape[0], STRIP):
        rows = pl.ds(start, STRIP)
        values = raw_ref[rows, :].astype(jnp.float32)
        scale = lax.rsqrt(jnp.sum(values * values, axis=1, keepdims=True) + EPSILON)
        unit_ref[rows, :] = (values * scale).astype(jnp.bfloat16)


def products_of(left, right):
    return lax.dot_general(
        left, right, (((1,), (1,)), ((), ())), preferred_element_type=jnp.float32
    )


def column_max(products):
    return jnp.max(products, axis=0, keepdims=True)


def row_max(products):
    width = products.shape[1]
    folded = products[:, :128]
    for start in range(128, width, 128):
        folded = jnp.maximum(folded, products[:, start : start + 128])
    return jnp.max(folded.T, axis=0, keepdims=True)


def own_kernel(raw_ref, unit_ref, high_ref):
    write_units(raw_ref, unit_ref)
    products = products_of(unit_ref[...], unit_ref[...])
    row = lax.broadcasted_iota(jnp.int32, products.shape, 0)
    col = lax.broadcasted_iota(jnp.int32, products.shape, 1)
    high_ref[...] = column_max(jnp.where(row == col, LOWEST, products))


def other_kernel(flags_ref, raw_ref, own_ref, high_in_ref, unit_ref, high_ref):
    write_units(raw_ref, unit_ref)
    high_ref[...] = high_in_ref[...]

    @pl.when(flags_ref[0] == 1)
    def _():
        products = products_of(unit_ref[...], own_ref[...])
        high_ref[...] = jnp.maximum(high_ref[...], column_max(products))


def mate_kernel(
    flags_ref, raw_ref, other_ref, column_ref, core_ref,
    unit_ref, to_other_ref, to_mate_ref, to_core_ref,
):
    write_units(raw_ref, unit_ref)
    for line_ref in (to_other_ref, to_mate_ref, to_core_ref):
        line_ref[...] = jnp.full_like(line_ref, LOWEST)

    @pl.when(flags_ref[2] == 1)
    def _():
        products = products_of(other_ref[...], unit_ref[...])
        to_other_ref[...] = row_max(products)
        to_mate_ref[...] = column_max(products)

    for far_ref, slot, near_ref, line_ref in (
        (core_ref, 3, other_ref, to_other_ref),
        (core_ref, 4, unit_ref, to_mate_ref),
        (column_ref, 5, other_ref, to_other_ref),
        (column_ref, 6, unit_ref, to_mate_ref),
    ):

        @pl.when(flags_ref[slot] == 1)
        def _():
            products = products_of(far_ref[...], near_ref[...])
            line_ref[...] = jnp.maximum(line_ref[...], column_max(products))
            if slot == 3:
                to_core_ref[...] = row_max(products)


def last_kernel(flags_ref, mate_ref, own_ref, high_in_ref, high_ref):
    high_ref[...] = high_in_ref[...]

    @pl.when(flags_ref[1] == 1)
    def _():
        products = products_of(mate_ref[...], own_ref[...])
        high_ref[...] = jnp.maximum(high_ref[...], column_max(products))


VMEM = pl.BlockSpec(memory_space=pltpu.VMEM)
SMEM = pl.BlockSpec(memory_space=pltpu.SMEM)
PARAMS = pltpu.CompilerParams(vmem_limit_bytes=16 * 1024 * 1024)


def call(kernel, args, outs, scratch=(), flops=0):
    specs = [SMEM if a.ndim == 1 else VMEM for a in args]
    moved = sum(a.size * a.dtype.itemsize for a in args)
    return pl.pallas_call(
        kernel,
        in_specs=specs,
        out_specs=[VMEM] * len(outs),
        out_shape=[jax.ShapeDtypeStruct(*o) for o in outs],
        scratch_shapes=list(scratch),
        compiler_params=PARAMS,
        cost_estimate=pl.CostEstimate(flops=flops, bytes_accessed=moved, transcendentals=0),
    )(*args)


def shards(embeddings, cluster_blocks):
    block, width = embeddings.shape
    from_other = swapped(embeddings, other_neighbour)
    from_mate = swapped(embeddings, pair_mate)

    bounds = jnp.cumsum(cluster_blocks)
    me = lax.axis_index(AXES)
    odd = me % 2
    second = me // 4 % 2
    with_prev = joined(bounds, me - 1, 1)
    with_next = joined(bounds, me, 1)
    around = joined(bounds, me - 1, 2)
    before = joined(bounds, me - 4, 3)
    after = joined(bounds, me + 1, 3)
    with_core = jnp.where(second == 1, before, after)
    with_column = jnp.where(second == 1, after, before)
    core_to_mate = jnp.where(second == 1, odd, 1 - odd)
    flags = jnp.stack(
        [
            jnp.where(odd == 1, with_next, with_prev),
            jnp.where(odd == 1, with_prev, with_next),
            around,
            with_core * (1 - core_to_mate),
            with_core * core_to_mate,
            with_column * core_to_mate,
            with_column * (1 - core_to_mate),
        ]
    )
    units = ((block, width), jnp.bfloat16)
    line = ((1, block), jnp.float32)
    tile = 2 * block * block * width

    own, high = call(own_kernel, (embeddings,), [units, line], flops=tile)
    column = swapped(own, column_neighbour)
    core = swapped(own, core_mate)
    other, high = call(other_kernel, (flags, from_other, own, high), [units, line], flops=tile)
    mate, to_other, to_mate, to_core = call(
        mate_kernel,
        (flags, from_mate, other, column, core),
        [units, line, line, line],
        flops=tile,
    )
    from_other = swapped(to_other, other_neighbour)
    from_mate = swapped(to_mate, pair_mate)
    from_core = swapped(to_core, to_the_ends)
    high = call(last_kernel, (flags, mate, own, high), [line], flops=tile)[0]
    at_end = (me == 0) | (me == lax.axis_size(AXES) - 1)
    returned = jnp.maximum(jnp.where(at_end, from_core, from_other), from_mate)
    return jnp.maximum(high, returned).reshape(block)


def solution(mesh):
    in_specs = (P(AXES, None), P())
    out_specs = P(AXES)
    return jax.shard_map(shards, mesh=mesh, in_specs=in_specs, out_specs=out_specs, check_vma=False)
```

```python
import jax
import jax.numpy as jnp
from jax import lax
from jax.experimental import pallas as pl
from jax.experimental.pallas import tpu as pltpu
from jax.sharding import PartitionSpec as P

EPSILON = 1e-06
AXES = ("rows", "bal")
LOWEST = -2.0
STRIP = 64


def pair_mate(i, n):
    return i ^ 1


def other_neighbour(i, n):
    return (i + 1) % n if i % 2 else (i - 1) % n


def core_mate(i, n):
    return i ^ 4


def column_neighbour(i, n):
    return (i + 4) % n if i // 4 % 2 else (i - 4) % n


def swapped(block, partner):
    n = lax.axis_size(AXES)
    pairs = [(i, partner(i, n)) for i in range(n)]
    return lax.ppermute(block, AXES, [p for p in pairs if p[1] is not None])


def joined(bounds, lower, distance):
    n = lax.axis_size(AXES)
    lower = lax.rem(lower + n, n)
    upper = lower + distance
    crossing = jnp.sum(((bounds > lower) & (bounds <= upper)).astype(jnp.int32))
    return ((upper < n) & (crossing == 0)).astype(jnp.int32)


def write_units(raw_ref, unit_ref):
    for start in range(0, raw_ref.shape[0], STRIP):
        rows = pl.ds(start, STRIP)
        values = raw_ref[rows, :].astype(jnp.float32)
        scale = lax.rsqrt(jnp.sum(values * values, axis=1, keepdims=True) + EPSILON)
        unit_ref[rows, :] = (values * scale).astype(jnp.bfloat16)


def products_of(left, right):
    return lax.dot_general(
        left, right, (((1,), (1,)), ((), ())), preferred_element_type=jnp.float32
    )


def column_max(products):
    return jnp.max(products, axis=0, keepdims=True)


def row_max(products):
    width = products.shape[1]
    folded = products[:, :128]
    for start in range(128, width, 128):
        folded = jnp.maximum(folded, products[:, start : start + 128])
    return jnp.max(folded.T, axis=0, keepdims=True)


def own_kernel(raw_ref, unit_ref, high_ref):
    write_units(raw_ref, unit_ref)
    products = products_of(unit_ref[...], unit_ref[...])
    row = lax.broadcasted_iota(jnp.int32, products.shape, 0)
    col = lax.broadcasted_iota(jnp.int32, products.shape, 1)
    high_ref[...] = column_max(jnp.where(row == col, LOWEST, products))


def other_kernel(flags_ref, raw_ref, own_ref, high_in_ref, unit_ref, high_ref):
    write_units(raw_ref, unit_ref)
    high_ref[...] = high_in_ref[...]

    @pl.when(flags_ref[0] == 1)
    def _():
        products = products_of(unit_ref[...], own_ref[...])
        high_ref[...] = jnp.maximum(high_ref[...], column_max(products))


def mate_kernel(flags_ref, raw_ref, other_ref, unit_ref, to_other_ref, to_mate_ref):
    write_units(raw_ref, unit_ref)
    to_other_ref[...] = jnp.full_like(to_other_ref, LOWEST)
    to_mate_ref[...] = jnp.full_like(to_mate_ref, LOWEST)

    @pl.when(flags_ref[2] == 1)
    def _():
        products = products_of(other_ref[...], unit_ref[...])
        to_other_ref[...] = row_max(products)
        to_mate_ref[...] = column_max(products)


def far_kernel(
    flags_ref, core_ref, column_ref, other_ref, mate_ref, other_in_ref, mate_in_ref,
    to_other_ref, to_mate_ref,
):
    to_other_ref[...] = other_in_ref[...]
    to_mate_ref[...] = mate_in_ref[...]
    for far_ref, slot, near_ref, line_ref in (
        (core_ref, 3, other_ref, to_other_ref),
        (core_ref, 4, mate_ref, to_mate_ref),
        (column_ref, 5, other_ref, to_other_ref),
        (column_ref, 6, mate_ref, to_mate_ref),
    ):

        @pl.when(flags_ref[slot] == 1)
        def _():
            products = products_of(far_ref[...], near_ref[...])
            line_ref[...] = jnp.maximum(line_ref[...], column_max(products))


def last_kernel(flags_ref, mate_ref, own_ref, high_in_ref, high_ref):
    high_ref[...] = high_in_ref[...]

    @pl.when(flags_ref[1] == 1)
    def _():
        products = products_of(mate_ref[...], own_ref[...])
        high_ref[...] = jnp.maximum(high_ref[...], column_max(products))


VMEM = pl.BlockSpec(memory_space=pltpu.VMEM)
SMEM = pl.BlockSpec(memory_space=pltpu.SMEM)
PARAMS = pltpu.CompilerParams(vmem_limit_bytes=16 * 1024 * 1024)


def call(kernel, args, outs, scratch=(), flops=0):
    specs = [SMEM if a.ndim == 1 else VMEM for a in args]
    moved = sum(a.size * a.dtype.itemsize for a in args)
    return pl.pallas_call(
        kernel,
        in_specs=specs,
        out_specs=[VMEM] * len(outs),
        out_shape=[jax.ShapeDtypeStruct(*o) for o in outs],
        scratch_shapes=list(scratch),
        compiler_params=PARAMS,
        cost_estimate=pl.CostEstimate(flops=flops, bytes_accessed=moved, transcendentals=0),
    )(*args)


def shards(embeddings, cluster_blocks):
    block, width = embeddings.shape
    from_other = swapped(embeddings, other_neighbour)
    from_mate = swapped(embeddings, pair_mate)

    bounds = jnp.cumsum(cluster_blocks)
    me = lax.axis_index(AXES)
    odd = me % 2
    second = me // 4 % 2
    with_prev = joined(bounds, me - 1, 1)
    with_next = joined(bounds, me, 1)
    around = joined(bounds, me - 1, 2)
    before = joined(bounds, me - 4, 3)
    after = joined(bounds, me + 1, 3)
    with_core = jnp.where(second == 1, before, after)
    with_column = jnp.where(second == 1, after, before)
    core_to_mate = jnp.where(second == 1, odd, 1 - odd)
    flags = jnp.stack(
        [
            jnp.where(odd == 1, with_next, with_prev),
            jnp.where(odd == 1, with_prev, with_next),
            around,
            with_core * (1 - core_to_mate),
            with_core * core_to_mate,
            with_column * core_to_mate,
            with_column * (1 - core_to_mate),
        ]
    )
    units = ((block, width), jnp.bfloat16)
    line = ((1, block), jnp.float32)
    tile = 2 * block * block * width

    own, high = call(own_kernel, (embeddings,), [units, line], flops=tile)
    column = swapped(own, column_neighbour)
    core = swapped(own, core_mate)
    other, high = call(other_kernel, (flags, from_other, own, high), [units, line], flops=tile)
    mate, to_other, to_mate = call(
        mate_kernel, (flags, from_mate, other), [units, line, line], flops=tile
    )
    to_other, to_mate = call(
        far_kernel,
        (flags, core, column, other, mate, to_other, to_mate),
        [line, line],
        flops=tile,
    )
    returned = swapped(to_other, other_neighbour), swapped(to_mate, pair_mate)
    high = call(last_kernel, (flags, mate, own, high), [line], flops=tile)[0]
    returned = jnp.maximum(*returned)
    return jnp.maximum(high, returned).reshape(block)


def solution(mesh):
    in_specs = (P(AXES, None), P())
    out_specs = P(AXES)
    return jax.shard_map(shards, mesh=mesh, in_specs=in_specs, out_specs=out_specs, check_vma=False)
```

```python
import jax
import jax.numpy as jnp
from jax import lax
from jax.experimental import pallas as pl
from jax.experimental.pallas import tpu as pltpu
from jax.sharding import PartitionSpec as P

EPSILON = 1e-06
AXES = ("rows", "bal")
LOWEST = -2.0
STRIP = 64
FETCHES = 4


def pair_mate(i, n):
    return i ^ 1


def other_neighbour(i, n):
    return (i + 1) % n if i % 2 else (i - 1) % n


def core_mate(i, n):
    return i ^ 4


def column_neighbour(i, n):
    j = i + 4 if i // 4 % 2 else i - 4
    return j if 0 <= j < n else None


def to_the_ends(i, n):
    return {4: 0, n - 5: n - 1}.get(i)


def swapped(block, partner):
    n = lax.axis_size(AXES)
    pairs = [(i, partner(i, n)) for i in range(n)]
    return lax.ppermute(block, AXES, [p for p in pairs if p[1] is not None])


def joined(bounds, lower, distance):
    upper = lower + distance
    crossing = jnp.sum(((bounds > lower) & (bounds <= upper)).astype(jnp.int32))
    inside = (lower >= 0) & (upper < lax.axis_size(AXES))
    return (inside & (crossing == 0)).astype(jnp.int32)


def write_units(raw_ref, unit_ref):
    for start in range(0, raw_ref.shape[0], STRIP):
        rows = pl.ds(start, STRIP)
        values = raw_ref[rows, :].astype(jnp.float32)
        scale = lax.rsqrt(jnp.sum(values * values, axis=1, keepdims=True) + EPSILON)
        unit_ref[rows, :] = (values * scale).astype(jnp.bfloat16)


def fetch_units(raw_ref, stage_ref, sems, unit_ref):
    rows = stage_ref.shape[0] // FETCHES
    copies = [
        pltpu.make_async_copy(
            raw_ref.at[pl.ds(i * rows, rows)], stage_ref.at[pl.ds(i * rows, rows)], sems.at[i]
        )
        for i in range(FETCHES)
    ]
    for copy in copies:
        copy.start()
    for i, copy in enumerate(copies):
        copy.wait()
        part = pl.ds(i * rows, rows)
        write_units(stage_ref.at[part], unit_ref.at[part])


def products_of(left, right):
    return lax.dot_general(
        left, right, (((1,), (1,)), ((), ())), preferred_element_type=jnp.float32
    )


def column_max(products):
    return jnp.max(products, axis=0, keepdims=True)


def row_max(products):
    width = products.shape[1]
    folded = products[:, :128]
    for start in range(128, width, 128):
        folded = jnp.maximum(folded, products[:, start : start + 128])
    return jnp.max(folded.T, axis=0, keepdims=True)


def own_kernel(raw_ref, unit_ref, high_ref, stage_ref, sems):
    fetch_units(raw_ref, stage_ref, sems, unit_ref)
    products = products_of(unit_ref[...], unit_ref[...])
    row = lax.broadcasted_iota(jnp.int32, products.shape, 0)
    col = lax.broadcasted_iota(jnp.int32, products.shape, 1)
    high_ref[...] = column_max(jnp.where(row == col, LOWEST, products))


def near_kernel(flags_ref, raw_ref, own_ref, high_in_ref, unit_ref, high_ref):
    write_units(raw_ref, unit_ref)
    high_ref[...] = high_in_ref[...]

    @pl.when(flags_ref[0, 0] == 1)
    def _():
        products = products_of(unit_ref[...], own_ref[...])
        high_ref[...] = jnp.maximum(high_ref[...], column_max(products))


def between_kernel(flags_ref, raw_ref, mate_ref, unit_ref, to_other_ref, to_mate_ref):
    write_units(raw_ref, unit_ref)
    to_other_ref[...] = jnp.full_like(to_other_ref, LOWEST)
    to_mate_ref[...] = jnp.full_like(to_mate_ref, LOWEST)

    @pl.when(flags_ref[0, 2] == 1)
    def _():
        products = products_of(mate_ref[...], unit_ref[...])
        to_mate_ref[...] = row_max(products)
        to_other_ref[...] = column_max(products)


def far_kernel(
    flags_ref, core_ref, column_ref, other_ref, mate_ref, other_in_ref, mate_in_ref,
    to_other_ref, to_mate_ref, to_core_ref, stage_ref, sems,
):
    to_other_ref[...] = other_in_ref[...]
    to_mate_ref[...] = mate_in_ref[...]
    to_core_ref[...] = jnp.full_like(to_core_ref, LOWEST)
    for i, (far_ref, slot) in enumerate(((core_ref, 3), (column_ref, 5))):

        @pl.when(flags_ref[0, slot] + flags_ref[0, slot + 1] > 0)
        def _():
            pltpu.make_async_copy(far_ref, stage_ref.at[i], sems.at[i]).start()

    for i, (far_ref, slot) in enumerate(((core_ref, 3), (column_ref, 5))):

        @pl.when(flags_ref[0, slot] + flags_ref[0, slot + 1] > 0)
        def _():
            pltpu.make_async_copy(far_ref, stage_ref.at[i], sems.at[i]).wait()

        for near_ref, line_ref, flag in (
            (other_ref, to_other_ref, flags_ref[0, slot]),
            (mate_ref, to_mate_ref, flags_ref[0, slot + 1]),
        ):

            @pl.when(flag == 1)
            def _():
                products = products_of(stage_ref[i], near_ref[...])
                line_ref[...] = jnp.maximum(line_ref[...], column_max(products))
                if far_ref is core_ref and near_ref is other_ref:
                    to_core_ref[...] = row_max(products)


def last_kernel(flags_ref, other_ref, own_ref, high_in_ref, high_ref):
    high_ref[...] = high_in_ref[...]

    @pl.when(flags_ref[0, 1] == 1)
    def _():
        products = products_of(other_ref[...], own_ref[...])
        high_ref[...] = jnp.maximum(high_ref[...], column_max(products))


VMEM = pl.BlockSpec(memory_space=pltpu.VMEM)
PARAMS = pltpu.CompilerParams(vmem_limit_bytes=16 * 1024 * 1024)


def call(kernel, args, outs, scratch=(), flops=0, aliases=None, in_hbm=()):
    specs = [VMEM] * len(args)
    for i in in_hbm:
        specs[i] = pl.BlockSpec(memory_space=pltpu.HBM)
    moved = sum(a.size * a.dtype.itemsize for a in args)
    return pl.pallas_call(
        kernel,
        in_specs=specs,
        out_specs=[VMEM] * len(outs),
        out_shape=[jax.ShapeDtypeStruct(*o) for o in outs],
        scratch_shapes=list(scratch),
        input_output_aliases=aliases or {},
        compiler_params=PARAMS,
        cost_estimate=pl.CostEstimate(flops=flops, bytes_accessed=moved, transcendentals=0),
    )(*args)


def shards(embeddings, cluster_blocks):
    block, width = embeddings.shape
    from_other = swapped(embeddings, other_neighbour)
    from_mate = swapped(embeddings, pair_mate)

    bounds = jnp.cumsum(cluster_blocks)
    me = lax.axis_index(AXES)
    odd = me % 2
    second = me // 4 % 2
    with_prev = joined(bounds, me - 1, 1)
    with_next = joined(bounds, me, 1)
    around = joined(bounds, me - 1, 2)
    before = joined(bounds, me - 4, 3)
    after = joined(bounds, me + 1, 3)
    with_core = jnp.where(second == 1, before, after)
    with_column = jnp.where(second == 1, after, before)
    core_to_mate = jnp.where(second == 1, odd, 1 - odd)
    flags = jnp.stack(
        [
            jnp.where(odd == 1, with_prev, with_next),
            jnp.where(odd == 1, with_next, with_prev),
            around,
            with_core * (1 - core_to_mate),
            with_core * core_to_mate,
            with_column * core_to_mate,
            with_column * (1 - core_to_mate),
            jnp.zeros_like(me),
        ]
    )[None, :]
    units = ((block, width), jnp.bfloat16)
    line = ((1, block), jnp.float32)
    tile = 2 * block * block * width

    stage = [pltpu.VMEM(*units), pltpu.SemaphoreType.DMA((FETCHES,))]
    own, high = call(own_kernel, (embeddings,), [units, line], stage, flops=tile, in_hbm=(0,))
    column = swapped(own, column_neighbour)
    core = swapped(own, core_mate)
    mate, high = call(
        near_kernel, (flags, from_mate, own, high), [units, line], flops=tile, aliases={1: 0}
    )
    other, to_other, to_mate = call(
        between_kernel, (flags, from_other, mate), [units, line, line], flops=tile, aliases={1: 0}
    )
    both = [pltpu.VMEM((2, block, width), jnp.bfloat16), pltpu.SemaphoreType.DMA((2,))]
    to_other, to_mate, to_core = call(
        far_kernel,
        (flags, core, column, other, mate, to_other, to_mate),
        [line, line, line],
        both,
        flops=tile,
        in_hbm=(1, 2),
    )
    from_other = swapped(to_other, other_neighbour)
    from_mate = swapped(to_mate, pair_mate)
    from_core = swapped(to_core, to_the_ends)
    high = call(last_kernel, (flags, other, own, high), [line], flops=tile)[0]
    at_end = (me == 0) | (me == lax.axis_size(AXES) - 1)
    returned = jnp.maximum(jnp.where(at_end, from_core, from_other), from_mate)
    return jnp.maximum(high, returned).reshape(block)


def solution(mesh):
    in_specs = (P(AXES, None), P())
    out_specs = P(AXES)
    return jax.shard_map(shards, mesh=mesh, in_specs=in_specs, out_specs=out_specs, check_vma=False)
```

```python
import jax
import jax.numpy as jnp
from jax import lax
from jax.experimental import pallas as pl
from jax.experimental.pallas import tpu as pltpu
from jax.sharding import PartitionSpec as P

EPSILON = 1e-06
AXES = ("rows", "bal")
LOWEST = -2.0
STRIP = 64
FETCHES = 4


def pair_mate(i, n):
    return i ^ 1


def other_neighbour(i, n):
    return (i + 1) % n if i % 2 else (i - 1) % n


def core_mate(i, n):
    return i ^ 4


def column_neighbour(i, n):
    j = i + 4 if i // 4 % 2 else i - 4
    return j if 0 <= j < n else None


def return_to_other(i, n):
    return {4: 0, 0: 3, n - 5: n - 1, n - 1: n - 4}.get(i, other_neighbour(i, n))


def beside_the_ends(i, n):
    return {4: 3, n - 5: n - 4}.get(i)


def swapped(block, partner):
    n = lax.axis_size(AXES)
    pairs = [(i, partner(i, n)) for i in range(n)]
    return lax.ppermute(block, AXES, [p for p in pairs if p[1] is not None])


def joined(bounds, lower, distance):
    upper = lower + distance
    crossing = jnp.sum(((bounds > lower) & (bounds <= upper)).astype(jnp.int32))
    inside = (lower >= 0) & (upper < lax.axis_size(AXES))
    return (inside & (crossing == 0)).astype(jnp.int32)


def write_units(raw_ref, unit_ref):
    for start in range(0, raw_ref.shape[0], STRIP):
        rows = pl.ds(start, STRIP)
        values = raw_ref[rows, :].astype(jnp.float32)
        scale = lax.rsqrt(jnp.sum(values * values, axis=1, keepdims=True) + EPSILON)
        unit_ref[rows, :] = (values * scale).astype(jnp.bfloat16)


def fetch_units(raw_ref, stage_ref, sems, unit_ref):
    rows = stage_ref.shape[0] // FETCHES
    copies = [
        pltpu.make_async_copy(
            raw_ref.at[pl.ds(i * rows, rows)], stage_ref.at[pl.ds(i * rows, rows)], sems.at[i]
        )
        for i in range(FETCHES)
    ]
    for copy in copies:
        copy.start()
    for i, copy in enumerate(copies):
        copy.wait()
        part = pl.ds(i * rows, rows)
        write_units(stage_ref.at[part], unit_ref.at[part])


def products_of(left, right):
    return lax.dot_general(
        left, right, (((1,), (1,)), ((), ())), preferred_element_type=jnp.float32
    )


def column_max(products):
    return jnp.max(products, axis=0, keepdims=True)


def row_max(products):
    width = products.shape[1]
    folded = products[:, :128]
    for start in range(128, width, 128):
        folded = jnp.maximum(folded, products[:, start : start + 128])
    return jnp.max(folded.T, axis=0, keepdims=True)


def own_kernel(raw_ref, unit_ref, high_ref, stage_ref, sems):
    fetch_units(raw_ref, stage_ref, sems, unit_ref)
    products = products_of(unit_ref[...], unit_ref[...])
    row = lax.broadcasted_iota(jnp.int32, products.shape, 0)
    col = lax.broadcasted_iota(jnp.int32, products.shape, 1)
    high_ref[...] = column_max(jnp.where(row == col, LOWEST, products))


def near_kernel(flags_ref, raw_ref, own_ref, high_in_ref, unit_ref, high_ref):
    write_units(raw_ref, unit_ref)
    high_ref[...] = high_in_ref[...]

    @pl.when(flags_ref[0, 0] == 1)
    def _():
        products = products_of(unit_ref[...], own_ref[...])
        high_ref[...] = jnp.maximum(high_ref[...], column_max(products))


def between_kernel(flags_ref, raw_ref, mate_ref, unit_ref, to_other_ref, to_mate_ref):
    write_units(raw_ref, unit_ref)
    to_other_ref[...] = jnp.full_like(to_other_ref, LOWEST)
    to_mate_ref[...] = jnp.full_like(to_mate_ref, LOWEST)

    @pl.when(flags_ref[0, 2] == 1)
    def _():
        products = products_of(mate_ref[...], unit_ref[...])
        to_mate_ref[...] = row_max(products)
        to_other_ref[...] = column_max(products)


def far_kernel(
    flags_ref, core_ref, column_ref, other_ref, mate_ref, other_in_ref, mate_in_ref,
    first_ref, to_mate_ref, to_other_ref, to_core_ref, stage_ref, sems,
):
    to_other_ref[...] = other_in_ref[...]
    to_mate_ref[...] = mate_in_ref[...]
    to_core_ref[...] = jnp.full_like(to_core_ref, LOWEST)
    for i, (far_ref, slot) in enumerate(((core_ref, 3), (column_ref, 5))):

        @pl.when(flags_ref[0, slot] + flags_ref[0, slot + 1] > 0)
        def _():
            pltpu.make_async_copy(far_ref, stage_ref.at[i], sems.at[i]).start()

    for i, (far_ref, slot) in enumerate(((core_ref, 3), (column_ref, 5))):

        @pl.when(flags_ref[0, slot] + flags_ref[0, slot + 1] > 0)
        def _():
            pltpu.make_async_copy(far_ref, stage_ref.at[i], sems.at[i]).wait()

        for near_ref, line_ref, flag in (
            (other_ref, to_other_ref, flags_ref[0, slot]),
            (mate_ref, to_mate_ref, flags_ref[0, slot + 1]),
        ):

            @pl.when(flag == 1)
            def _():
                products = products_of(stage_ref[i], near_ref[...])
                line_ref[...] = jnp.maximum(line_ref[...], column_max(products))
                if far_ref is core_ref and near_ref is other_ref:
                    to_core_ref[...] = row_max(products)
    first_ref[...] = to_other_ref[...]

    @pl.when(flags_ref[0, 7] == 1)
    def _():
        first_ref[...] = to_core_ref[...]


def last_kernel(flags_ref, other_ref, own_ref, high_in_ref, high_ref):
    high_ref[...] = high_in_ref[...]

    @pl.when(flags_ref[0, 1] == 1)
    def _():
        products = products_of(other_ref[...], own_ref[...])
        high_ref[...] = jnp.maximum(high_ref[...], column_max(products))


VMEM = pl.BlockSpec(memory_space=pltpu.VMEM)
PARAMS = pltpu.CompilerParams(vmem_limit_bytes=16 * 1024 * 1024)


def call(kernel, args, outs, scratch=(), flops=0, aliases=None, in_hbm=()):
    specs = [VMEM] * len(args)
    for i in in_hbm:
        specs[i] = pl.BlockSpec(memory_space=pltpu.HBM)
    moved = sum(a.size * a.dtype.itemsize for a in args)
    return pl.pallas_call(
        kernel,
        in_specs=specs,
        out_specs=[VMEM] * len(outs),
        out_shape=[jax.ShapeDtypeStruct(*o) for o in outs],
        scratch_shapes=list(scratch),
        input_output_aliases=aliases or {},
        compiler_params=PARAMS,
        cost_estimate=pl.CostEstimate(flops=flops, bytes_accessed=moved, transcendentals=0),
    )(*args)


def shards(embeddings, cluster_blocks):
    block, width = embeddings.shape
    from_other = swapped(embeddings, other_neighbour)
    from_mate = swapped(embeddings, pair_mate)

    bounds = jnp.cumsum(cluster_blocks)
    me = lax.axis_index(AXES)
    odd = me % 2
    second = me // 4 % 2
    with_prev = joined(bounds, me - 1, 1)
    with_next = joined(bounds, me, 1)
    around = joined(bounds, me - 1, 2)
    before = joined(bounds, me - 4, 3)
    after = joined(bounds, me + 1, 3)
    blocks = lax.axis_size(AXES)
    serves_end = (me == 4) | (me == blocks - 5)
    with_core = jnp.where(second == 1, before, after)
    with_column = jnp.where(second == 1, after, before)
    core_to_mate = jnp.where(second == 1, odd, 1 - odd)
    flags = jnp.stack(
        [
            jnp.where(odd == 1, with_prev, with_next),
            jnp.where(odd == 1, with_next, with_prev),
            around,
            with_core * (1 - core_to_mate),
            with_core * core_to_mate,
            with_column * core_to_mate,
            with_column * (1 - core_to_mate),
            serves_end.astype(jnp.int32),
        ]
    )[None, :]
    units = ((block, width), jnp.bfloat16)
    line = ((1, block), jnp.float32)
    tile = 2 * block * block * width

    stage = [pltpu.VMEM(*units), pltpu.SemaphoreType.DMA((FETCHES,))]
    own, high = call(own_kernel, (embeddings,), [units, line], stage, flops=tile, in_hbm=(0,))
    column = swapped(own, column_neighbour)
    core = swapped(own, core_mate)
    mate, high = call(
        near_kernel, (flags, from_mate, own, high), [units, line], flops=tile, aliases={1: 0}
    )
    other, to_other, to_mate = call(
        between_kernel, (flags, from_other, mate), [units, line, line], flops=tile, aliases={1: 0}
    )
    both = [
        pltpu.VMEM(*line),
        pltpu.VMEM((2, block, width), jnp.bfloat16),
        pltpu.SemaphoreType.DMA((2,)),
    ]
    first, to_mate, to_other = call(
        far_kernel,
        (flags, core, column, other, mate, to_other, to_mate),
        [line, line, line],
        both,
        flops=tile,
        in_hbm=(1, 2),
    )
    from_first = swapped(first, return_to_other)
    from_mate = swapped(to_mate, pair_mate)
    from_beside = swapped(to_other, beside_the_ends)
    high = call(last_kernel, (flags, other, own, high), [line], flops=tile)[0]
    beside_end = (me == 3) | (me == blocks - 4)
    returned = jnp.maximum(jnp.where(beside_end, LOWEST, from_first), from_mate)
    rest = jnp.where(beside_end, from_beside, LOWEST)
    return jnp.maximum(jnp.maximum(high, returned), rest).reshape(block)


def solution(mesh):
    in_specs = (P(AXES, None), P())
    out_specs = P(AXES)
    return jax.shard_map(shards, mesh=mesh, in_specs=in_specs, out_specs=out_specs, check_vma=False)
```

```python
import jax
import jax.numpy as jnp
from jax import lax
from jax.experimental import pallas as pl
from jax.experimental.pallas import tpu as pltpu
from jax.sharding import PartitionSpec as P

EPSILON = 1e-06
AXES = ("rows", "bal")
LOWEST = -2.0
STRIP = 64
FETCHES = 4


def pair_mate(i, n):
    return i ^ 1


def other_neighbour(i, n):
    return (i + 1) % n if i % 2 else (i - 1) % n


def core_mate(i, n):
    return i ^ 4


def column_neighbour(i, n):
    j = i + 4 if i // 4 % 2 else i - 4
    return j if 0 <= j < n else None


def return_to_other(i, n):
    return {4: 0, 0: 3, n - 5: n - 1, n - 1: n - 4}.get(i, other_neighbour(i, n))


def beside_the_ends(i, n):
    return {4: 3, n - 5: n - 4}.get(i)


def swapped(block, partner):
    n = lax.axis_size(AXES)
    pairs = [(i, partner(i, n)) for i in range(n)]
    return lax.ppermute(block, AXES, [p for p in pairs if p[1] is not None])


def joined(bounds, lower, distance):
    upper = lower + distance
    crossing = jnp.sum(((bounds > lower) & (bounds <= upper)).astype(jnp.int32))
    inside = (lower >= 0) & (upper < lax.axis_size(AXES))
    return (inside & (crossing == 0)).astype(jnp.int32)


def write_units(raw_ref, unit_ref):
    for start in range(0, raw_ref.shape[0], STRIP):
        rows = pl.ds(start, STRIP)
        values = raw_ref[rows, :].astype(jnp.float32)
        scale = lax.rsqrt(jnp.sum(values * values, axis=1, keepdims=True) + EPSILON)
        unit_ref[rows, :] = (values * scale).astype(jnp.bfloat16)


def fetch_units(raw_ref, stage_ref, sems, unit_ref):
    rows = stage_ref.shape[0] // FETCHES
    copies = [
        pltpu.make_async_copy(
            raw_ref.at[pl.ds(i * rows, rows)], stage_ref.at[pl.ds(i * rows, rows)], sems.at[i]
        )
        for i in range(FETCHES)
    ]
    for copy in copies:
        copy.start()
    for i, copy in enumerate(copies):
        copy.wait()
        part = pl.ds(i * rows, rows)
        write_units(stage_ref.at[part], unit_ref.at[part])


def products_of(left, right):
    return lax.dot_general(
        left, right, (((1,), (1,)), ((), ())), preferred_element_type=jnp.float32
    )


def column_max(products):
    return jnp.max(products, axis=0, keepdims=True)


def row_max(products):
    width = products.shape[1]
    folded = products[:, :128]
    for start in range(128, width, 128):
        folded = jnp.maximum(folded, products[:, start : start + 128])
    return jnp.max(folded.T, axis=0, keepdims=True)


def own_kernel(raw_ref, unit_ref, high_ref, stage_ref, sems):
    fetch_units(raw_ref, stage_ref, sems, unit_ref)
    products = products_of(unit_ref[...], unit_ref[...])
    row = lax.broadcasted_iota(jnp.int32, products.shape, 0)
    col = lax.broadcasted_iota(jnp.int32, products.shape, 1)
    high_ref[...] = column_max(jnp.where(row == col, LOWEST, products))


def near_kernel(flags_ref, raw_ref, own_ref, high_in_ref, unit_ref, high_ref):
    write_units(raw_ref, unit_ref)
    high_ref[...] = high_in_ref[...]

    @pl.when(flags_ref[0, 0] == 1)
    def _():
        products = products_of(unit_ref[...], own_ref[...])
        high_ref[...] = jnp.maximum(high_ref[...], column_max(products))


def between_kernel(flags_ref, raw_ref, mate_ref, unit_ref, to_other_ref, to_mate_ref):
    write_units(raw_ref, unit_ref)
    to_other_ref[...] = jnp.full_like(to_other_ref, LOWEST)
    to_mate_ref[...] = jnp.full_like(to_mate_ref, LOWEST)

    @pl.when(flags_ref[0, 2] == 1)
    def _():
        products = products_of(mate_ref[...], unit_ref[...])
        to_mate_ref[...] = row_max(products)
        to_other_ref[...] = column_max(products)


def far_kernel(
    flags_ref, column_ref, core_ref, other_ref, mate_ref, other_in_ref, mate_in_ref,
    first_ref, to_mate_ref, to_other_ref, to_core_ref, stage_ref, sems,
):
    to_other_ref[...] = other_in_ref[...]
    to_mate_ref[...] = mate_in_ref[...]
    to_core_ref[...] = jnp.full_like(to_core_ref, LOWEST)
    for i, (far_ref, slot) in enumerate(((core_ref, 3), (column_ref, 5))):

        @pl.when(flags_ref[0, slot] + flags_ref[0, slot + 1] > 0)
        def _():
            pltpu.make_async_copy(far_ref, stage_ref.at[i], sems.at[i]).start()

    for i, (far_ref, slot) in enumerate(((core_ref, 3), (column_ref, 5))):

        @pl.when(flags_ref[0, slot] + flags_ref[0, slot + 1] > 0)
        def _():
            pltpu.make_async_copy(far_ref, stage_ref.at[i], sems.at[i]).wait()

        for near_ref, line_ref, flag in (
            (other_ref, to_other_ref, flags_ref[0, slot]),
            (mate_ref, to_mate_ref, flags_ref[0, slot + 1]),
        ):

            @pl.when(flag == 1)
            def _():
                products = products_of(stage_ref[i], near_ref[...])
                line_ref[...] = jnp.maximum(line_ref[...], column_max(products))
                if far_ref is core_ref and near_ref is other_ref:
                    to_core_ref[...] = row_max(products)
    first_ref[...] = to_other_ref[...]

    @pl.when(flags_ref[0, 7] == 1)
    def _():
        first_ref[...] = to_core_ref[...]


def last_kernel(flags_ref, other_ref, own_ref, high_in_ref, high_ref):
    high_ref[...] = high_in_ref[...]

    @pl.when(flags_ref[0, 1] == 1)
    def _():
        products = products_of(other_ref[...], own_ref[...])
        high_ref[...] = jnp.maximum(high_ref[...], column_max(products))


VMEM = pl.BlockSpec(memory_space=pltpu.VMEM)
PARAMS = pltpu.CompilerParams(vmem_limit_bytes=16 * 1024 * 1024)


def call(kernel, args, outs, scratch=(), flops=0, aliases=None, in_hbm=()):
    specs = [VMEM] * len(args)
    for i in in_hbm:
        specs[i] = pl.BlockSpec(memory_space=pltpu.HBM)
    moved = sum(a.size * a.dtype.itemsize for a in args)
    return pl.pallas_call(
        kernel,
        in_specs=specs,
        out_specs=[VMEM] * len(outs),
        out_shape=[jax.ShapeDtypeStruct(*o) for o in outs],
        scratch_shapes=list(scratch),
        input_output_aliases=aliases or {},
        compiler_params=PARAMS,
        cost_estimate=pl.CostEstimate(flops=flops, bytes_accessed=moved, transcendentals=0),
    )(*args)


def shards(embeddings, cluster_blocks):
    block, width = embeddings.shape
    from_other = swapped(embeddings, other_neighbour)
    from_mate = swapped(embeddings, pair_mate)

    bounds = jnp.cumsum(cluster_blocks)
    me = lax.axis_index(AXES)
    odd = me % 2
    second = me // 4 % 2
    with_prev = joined(bounds, me - 1, 1)
    with_next = joined(bounds, me, 1)
    around = joined(bounds, me - 1, 2)
    before = joined(bounds, me - 4, 3)
    after = joined(bounds, me + 1, 3)
    blocks = lax.axis_size(AXES)
    serves_end = (me == 4) | (me == blocks - 5)
    with_core = jnp.where(second == 1, before, after)
    with_column = jnp.where(second == 1, after, before)
    core_to_mate = jnp.where(second == 1, odd, 1 - odd)
    flags = jnp.stack(
        [
            jnp.where(odd == 1, with_prev, with_next),
            jnp.where(odd == 1, with_next, with_prev),
            around,
            with_core * (1 - core_to_mate),
            with_core * core_to_mate,
            with_column * core_to_mate,
            with_column * (1 - core_to_mate),
            serves_end.astype(jnp.int32),
        ]
    )[None, :]
    units = ((block, width), jnp.bfloat16)
    line = ((1, block), jnp.float32)
    tile = 2 * block * block * width

    stage = [pltpu.VMEM(*units), pltpu.SemaphoreType.DMA((FETCHES,))]
    own, high = call(own_kernel, (embeddings,), [units, line], stage, flops=tile, in_hbm=(0,))
    column = swapped(own, column_neighbour)
    core = swapped(own, core_mate)
    mate, high = call(
        near_kernel, (flags, from_mate, own, high), [units, line], flops=tile, aliases={1: 0}
    )
    other, to_other, to_mate = call(
        between_kernel, (flags, from_other, mate), [units, line, line], flops=tile, aliases={1: 0}
    )
    both = [
        pltpu.VMEM(*line),
        pltpu.VMEM((2, block, width), jnp.bfloat16),
        pltpu.SemaphoreType.DMA((2,)),
    ]
    first, to_mate, to_other = call(
        far_kernel,
        (flags, column, core, other, mate, to_other, to_mate),
        [line, line, line],
        both,
        flops=tile,
        in_hbm=(1, 2),
    )
    from_first = swapped(first, return_to_other)
    from_mate = swapped(to_mate, pair_mate)
    from_beside = swapped(to_other, beside_the_ends)
    high = call(last_kernel, (flags, other, own, high), [line], flops=tile)[0]
    beside_end = (me == 3) | (me == blocks - 4)
    returned = jnp.maximum(jnp.where(beside_end, LOWEST, from_first), from_mate)
    rest = jnp.where(beside_end, from_beside, LOWEST)
    return jnp.maximum(jnp.maximum(high, returned), rest).reshape(block)


def solution(mesh):
    in_specs = (P(AXES, None), P())
    out_specs = P(AXES)
    return jax.shard_map(shards, mesh=mesh, in_specs=in_specs, out_specs=out_specs, check_vma=False)
```

```python
import jax
import jax.numpy as jnp
from jax import lax
from jax.experimental import pallas as pl
from jax.experimental.pallas import tpu as pltpu
from jax.sharding import PartitionSpec as P

EPSILON = 1e-06
AXES = ("rows", "bal")
LOWEST = -2.0
STRIP = 64


def pair_mate(i, n):
    return i ^ 1


def other_neighbour(i, n):
    return (i + 1) % n if i % 2 else (i - 1) % n


def core_mate(i, n):
    return i ^ 4


def column_neighbour(i, n):
    j = i + 4 if i // 4 % 2 else i - 4
    return j if 0 <= j < n else None


def return_to_other(i, n):
    return {4: 0, 0: 3, n - 5: n - 1, n - 1: n - 4}.get(i, other_neighbour(i, n))


def beside_the_ends(i, n):
    return {4: 3, n - 5: n - 4}.get(i)


def swapped(block, partner):
    n = lax.axis_size(AXES)
    pairs = [(i, partner(i, n)) for i in range(n)]
    return lax.ppermute(block, AXES, [p for p in pairs if p[1] is not None])


def joined(bounds, lower, distance):
    upper = lower + distance
    crossing = jnp.sum(((bounds > lower) & (bounds <= upper)).astype(jnp.int32))
    inside = (lower >= 0) & (upper < lax.axis_size(AXES))
    return (inside & (crossing == 0)).astype(jnp.int32)


def write_units(raw_ref, unit_ref):
    for start in range(0, raw_ref.shape[0], STRIP):
        rows = pl.ds(start, STRIP)
        values = raw_ref[rows, :].astype(jnp.float32)
        scale = lax.rsqrt(jnp.sum(values * values, axis=1, keepdims=True) + EPSILON)
        unit_ref[rows, :] = (values * scale).astype(jnp.bfloat16)


def products_of(left, right):
    return lax.dot_general(
        left, right, (((1,), (1,)), ((), ())), preferred_element_type=jnp.float32
    )


def column_max(products):
    return jnp.max(products, axis=0, keepdims=True)


def row_max(products):
    width = products.shape[1]
    folded = products[:, :128]
    for start in range(128, width, 128):
        folded = jnp.maximum(folded, products[:, start : start + 128])
    return jnp.max(folded.T, axis=0, keepdims=True)


def own_kernel(raw_ref, unit_ref, high_ref):
    write_units(raw_ref, unit_ref)
    products = products_of(unit_ref[...], unit_ref[...])
    row = lax.broadcasted_iota(jnp.int32, products.shape, 0)
    col = lax.broadcasted_iota(jnp.int32, products.shape, 1)
    high_ref[...] = column_max(jnp.where(row == col, LOWEST, products))


def near_kernel(flags_ref, raw_ref, own_ref, high_in_ref, unit_ref, high_ref):
    write_units(raw_ref, unit_ref)
    high_ref[...] = high_in_ref[...]

    @pl.when(flags_ref[0, 0] == 1)
    def _():
        products = products_of(unit_ref[...], own_ref[...])
        high_ref[...] = jnp.maximum(high_ref[...], column_max(products))


def between_kernel(flags_ref, raw_ref, mate_ref, unit_ref, to_other_ref, to_mate_ref):
    write_units(raw_ref, unit_ref)
    to_other_ref[...] = jnp.full_like(to_other_ref, LOWEST)
    to_mate_ref[...] = jnp.full_like(to_mate_ref, LOWEST)

    @pl.when(flags_ref[0, 2] == 1)
    def _():
        products = products_of(mate_ref[...], unit_ref[...])
        to_mate_ref[...] = row_max(products)
        to_other_ref[...] = column_max(products)


def far_kernel(
    flags_ref, column_ref, core_ref, other_ref, mate_ref, other_in_ref, mate_in_ref,
    first_ref, to_mate_ref, to_other_ref, to_core_ref, stage_ref, sems,
):
    to_other_ref[...] = other_in_ref[...]
    to_mate_ref[...] = mate_in_ref[...]
    to_core_ref[...] = jnp.full_like(to_core_ref, LOWEST)
    far = ((core_ref, 3), (column_ref, 5))

    def fetch(i):
        return pltpu.make_async_copy(far[i][0], stage_ref.at[i], sems.at[i])

    for i, (_, slot) in enumerate(far):

        @pl.when(flags_ref[0, slot] + flags_ref[0, slot + 1] > 0)
        def _():
            fetch(i).start()

    for i, (_, slot) in enumerate(far):

        @pl.when(flags_ref[0, slot] + flags_ref[0, slot + 1] > 0)
        def _():
            fetch(i).wait()

            @pl.when(flags_ref[0, slot] == 1)
            def _():
                products = products_of(stage_ref[i], other_ref[...])
                to_other_ref[...] = jnp.maximum(to_other_ref[...], column_max(products))
                if i == 0:
                    to_core_ref[...] = row_max(products)

            @pl.when(flags_ref[0, slot + 1] == 1)
            def _():
                products = products_of(stage_ref[i], mate_ref[...])
                to_mate_ref[...] = jnp.maximum(to_mate_ref[...], column_max(products))

    first_ref[...] = to_other_ref[...]

    @pl.when(flags_ref[0, 7] == 1)
    def _():
        first_ref[...] = to_core_ref[...]


def last_kernel(flags_ref, other_ref, own_ref, high_in_ref, high_ref):
    high_ref[...] = high_in_ref[...]

    @pl.when(flags_ref[0, 1] == 1)
    def _():
        products = products_of(other_ref[...], own_ref[...])
        high_ref[...] = jnp.maximum(high_ref[...], column_max(products))


VMEM = pl.BlockSpec(memory_space=pltpu.VMEM)
PARAMS = pltpu.CompilerParams(vmem_limit_bytes=16 * 1024 * 1024)


def call(kernel, args, outs, scratch=(), flops=0, aliases=None, in_hbm=()):
    specs = [VMEM] * len(args)
    for i in in_hbm:
        specs[i] = pl.BlockSpec(memory_space=pltpu.HBM)
    moved = sum(a.size * a.dtype.itemsize for a in args)
    return pl.pallas_call(
        kernel,
        in_specs=specs,
        out_specs=[VMEM] * len(outs),
        out_shape=[jax.ShapeDtypeStruct(*o) for o in outs],
        scratch_shapes=list(scratch),
        input_output_aliases=aliases or {},
        compiler_params=PARAMS,
        cost_estimate=pl.CostEstimate(flops=flops, bytes_accessed=moved, transcendentals=0),
    )(*args)


def shards(embeddings, cluster_blocks):
    block, width = embeddings.shape
    from_other = swapped(embeddings, other_neighbour)
    from_mate = swapped(embeddings, pair_mate)

    bounds = jnp.cumsum(cluster_blocks)
    me = lax.axis_index(AXES)
    odd = me % 2
    second = me // 4 % 2
    with_prev = joined(bounds, me - 1, 1)
    with_next = joined(bounds, me, 1)
    around = joined(bounds, me - 1, 2)
    before = joined(bounds, me - 4, 3)
    after = joined(bounds, me + 1, 3)
    blocks = lax.axis_size(AXES)
    serves_end = (me == 4) | (me == blocks - 5)
    with_core = jnp.where(second == 1, before, after)
    with_column = jnp.where(second == 1, after, before)
    core_to_mate = jnp.where(second == 1, odd, 1 - odd)
    flags = jnp.stack(
        [
            jnp.where(odd == 1, with_prev, with_next),
            jnp.where(odd == 1, with_next, with_prev),
            around,
            with_core * (1 - core_to_mate),
            with_core * core_to_mate,
            with_column * core_to_mate,
            with_column * (1 - core_to_mate),
            serves_end.astype(jnp.int32),
        ]
    )[None, :]
    units = ((block, width), jnp.bfloat16)
    line = ((1, block), jnp.float32)
    tile = 2 * block * block * width

    own, high = call(own_kernel, (embeddings,), [units, line], flops=tile)
    column = swapped(own, column_neighbour)
    core = swapped(own, core_mate)
    mate, high = call(
        near_kernel, (flags, from_mate, own, high), [units, line], flops=tile, aliases={1: 0}
    )
    other, to_other, to_mate = call(
        between_kernel, (flags, from_other, mate), [units, line, line], flops=tile, aliases={1: 0}
    )
    both = [
        pltpu.VMEM(*line),
        pltpu.VMEM((2, block, width), jnp.bfloat16),
        pltpu.SemaphoreType.DMA((2,)),
    ]
    first, to_mate, to_other = call(
        far_kernel,
        (flags, column, core, other, mate, to_other, to_mate),
        [line, line, line],
        both,
        flops=tile,
        in_hbm=(1, 2),
    )
    from_first = swapped(first, return_to_other)
    from_mate = swapped(to_mate, pair_mate)
    from_beside = swapped(to_other, beside_the_ends)
    high = call(last_kernel, (flags, other, own, high), [line], flops=tile)[0]
    beside_end = (me == 3) | (me == blocks - 4)
    returned = jnp.maximum(jnp.where(beside_end, LOWEST, from_first), from_mate)
    rest = jnp.where(beside_end, from_beside, LOWEST)
    return jnp.maximum(jnp.maximum(high, returned), rest).reshape(block)


def solution(mesh):
    in_specs = (P(AXES, None), P())
    out_specs = P(AXES)
    return jax.shard_map(shards, mesh=mesh, in_specs=in_specs, out_specs=out_specs, check_vma=False)
```

```python
import jax
import jax.numpy as jnp
from jax import lax
from jax.experimental import pallas as pl
from jax.experimental.pallas import tpu as pltpu
from jax.sharding import PartitionSpec as P

EPSILON = 1e-06
AXES = ("rows", "bal")
LOWEST = -2.0
STRIP = 32


def pair_mate(i, n):
    return i ^ 1


def other_neighbour(i, n):
    return (i + 1) % n if i % 2 else (i - 1) % n


def core_mate(i, n):
    return i ^ 4


def column_neighbour(i, n):
    j = i + 4 if i // 4 % 2 else i - 4
    return j if 0 <= j < n else None


def return_to_other(i, n):
    return {4: 0, 0: 3, n - 5: n - 1, n - 1: n - 4}.get(i, other_neighbour(i, n))


def beside_the_ends(i, n):
    return {4: 3, n - 5: n - 4}.get(i)


def swapped(block, partner):
    n = lax.axis_size(AXES)
    pairs = [(i, partner(i, n)) for i in range(n)]
    return lax.ppermute(block, AXES, [p for p in pairs if p[1] is not None])


def joined(bounds, lower, distance):
    upper = lower + distance
    crossing = jnp.sum(((bounds > lower) & (bounds <= upper)).astype(jnp.int32))
    inside = (lower >= 0) & (upper < lax.axis_size(AXES))
    return (inside & (crossing == 0)).astype(jnp.int32)


def write_units(raw_ref, unit_ref):
    for start in range(0, raw_ref.shape[0], STRIP):
        rows = pl.ds(start, STRIP)
        values = raw_ref[rows, :].astype(jnp.float32)
        scale = lax.rsqrt(jnp.sum(values * values, axis=1, keepdims=True) + EPSILON)
        unit_ref[rows, :] = (values * scale).astype(jnp.bfloat16)


def products_of(left, right):
    return lax.dot_general(
        left, right, (((1,), (1,)), ((), ())), preferred_element_type=jnp.float32
    )


def column_max(products):
    return jnp.max(products, axis=0, keepdims=True)


def row_max(products):
    width = products.shape[1]
    folded = products[:, :128]
    for start in range(128, width, 128):
        folded = jnp.maximum(folded, products[:, start : start + 128])
    return jnp.max(folded.T, axis=0, keepdims=True)


def own_kernel(raw_ref, unit_ref, high_ref):
    write_units(raw_ref, unit_ref)
    products = products_of(unit_ref[...], unit_ref[...])
    row = lax.broadcasted_iota(jnp.int32, products.shape, 0)
    col = lax.broadcasted_iota(jnp.int32, products.shape, 1)
    high_ref[...] = column_max(jnp.where(row == col, LOWEST, products))


def near_kernel(flags_ref, raw_ref, own_ref, high_in_ref, unit_ref, high_ref):
    write_units(raw_ref, unit_ref)
    high_ref[...] = high_in_ref[...]

    @pl.when(flags_ref[0, 0] == 1)
    def _():
        products = products_of(unit_ref[...], own_ref[...])
        high_ref[...] = jnp.maximum(high_ref[...], column_max(products))


def between_kernel(flags_ref, raw_ref, mate_ref, unit_ref, to_other_ref, to_mate_ref):
    write_units(raw_ref, unit_ref)
    to_other_ref[...] = jnp.full_like(to_other_ref, LOWEST)
    to_mate_ref[...] = jnp.full_like(to_mate_ref, LOWEST)

    @pl.when(flags_ref[0, 2] == 1)
    def _():
        products = products_of(mate_ref[...], unit_ref[...])
        to_mate_ref[...] = row_max(products)
        to_other_ref[...] = column_max(products)


def far_kernel(
    flags_ref, column_ref, core_ref, other_ref, mate_ref, other_in_ref, mate_in_ref,
    first_ref, to_mate_ref, to_other_ref, to_core_ref, stage_ref, sems,
):
    to_other_ref[...] = other_in_ref[...]
    to_mate_ref[...] = mate_in_ref[...]
    to_core_ref[...] = jnp.full_like(to_core_ref, LOWEST)
    far = ((core_ref, 3), (column_ref, 5))

    def fetch(i):
        return pltpu.make_async_copy(far[i][0], stage_ref.at[i], sems.at[i])

    for i, (_, slot) in enumerate(far):

        @pl.when(flags_ref[0, slot] + flags_ref[0, slot + 1] > 0)
        def _():
            fetch(i).start()

    for i, (_, slot) in enumerate(far):

        @pl.when(flags_ref[0, slot] + flags_ref[0, slot + 1] > 0)
        def _():
            fetch(i).wait()

            @pl.when(flags_ref[0, slot] == 1)
            def _():
                products = products_of(stage_ref[i], other_ref[...])
                to_other_ref[...] = jnp.maximum(to_other_ref[...], column_max(products))
                if i == 0:
                    to_core_ref[...] = row_max(products)

            @pl.when(flags_ref[0, slot + 1] == 1)
            def _():
                products = products_of(stage_ref[i], mate_ref[...])
                to_mate_ref[...] = jnp.maximum(to_mate_ref[...], column_max(products))

    first_ref[...] = to_other_ref[...]

    @pl.when(flags_ref[0, 7] == 1)
    def _():
        first_ref[...] = to_core_ref[...]


def last_kernel(flags_ref, other_ref, own_ref, high_in_ref, high_ref):
    high_ref[...] = high_in_ref[...]

    @pl.when(flags_ref[0, 1] == 1)
    def _():
        products = products_of(other_ref[...], own_ref[...])
        high_ref[...] = jnp.maximum(high_ref[...], column_max(products))


VMEM = pl.BlockSpec(memory_space=pltpu.VMEM)
PARAMS = pltpu.CompilerParams(vmem_limit_bytes=16 * 1024 * 1024)


def call(kernel, args, outs, scratch=(), flops=0, aliases=None, in_hbm=()):
    specs = [VMEM] * len(args)
    for i in in_hbm:
        specs[i] = pl.BlockSpec(memory_space=pltpu.HBM)
    moved = sum(a.size * a.dtype.itemsize for a in args)
    return pl.pallas_call(
        kernel,
        in_specs=specs,
        out_specs=[VMEM] * len(outs),
        out_shape=[jax.ShapeDtypeStruct(*o) for o in outs],
        scratch_shapes=list(scratch),
        input_output_aliases=aliases or {},
        compiler_params=PARAMS,
        cost_estimate=pl.CostEstimate(flops=flops, bytes_accessed=moved, transcendentals=0),
    )(*args)


def shards(embeddings, cluster_blocks):
    block, width = embeddings.shape
    from_other = swapped(embeddings, other_neighbour)
    from_mate = swapped(embeddings, pair_mate)

    bounds = jnp.cumsum(cluster_blocks)
    me = lax.axis_index(AXES)
    odd = me % 2
    second = me // 4 % 2
    with_prev = joined(bounds, me - 1, 1)
    with_next = joined(bounds, me, 1)
    around = joined(bounds, me - 1, 2)
    before = joined(bounds, me - 4, 3)
    after = joined(bounds, me + 1, 3)
    blocks = lax.axis_size(AXES)
    serves_end = (me == 4) | (me == blocks - 5)
    with_core = jnp.where(second == 1, before, after)
    with_column = jnp.where(second == 1, after, before)
    core_to_mate = jnp.where(second == 1, odd, 1 - odd)
    flags = jnp.stack(
        [
            jnp.where(odd == 1, with_prev, with_next),
            jnp.where(odd == 1, with_next, with_prev),
            around,
            with_core * (1 - core_to_mate),
            with_core * core_to_mate,
            with_column * core_to_mate,
            with_column * (1 - core_to_mate),
            serves_end.astype(jnp.int32),
        ]
    )[None, :]
    units = ((block, width), jnp.bfloat16)
    line = ((1, block), jnp.float32)
    tile = 2 * block * block * width

    own, high = call(own_kernel, (embeddings,), [units, line], flops=tile)
    column = swapped(own, column_neighbour)
    core = swapped(own, core_mate)
    mate, high = call(
        near_kernel, (flags, from_mate, own, high), [units, line], flops=tile, aliases={1: 0}
    )
    other, to_other, to_mate = call(
        between_kernel, (flags, from_other, mate), [units, line, line], flops=tile, aliases={1: 0}
    )
    both = [
        pltpu.VMEM(*line),
        pltpu.VMEM((2, block, width), jnp.bfloat16),
        pltpu.SemaphoreType.DMA((2,)),
    ]
    first, to_mate, to_other = call(
        far_kernel,
        (flags, column, core, other, mate, to_other, to_mate),
        [line, line, line],
        both,
        flops=tile,
        in_hbm=(1, 2),
    )
    from_first = swapped(first, return_to_other)
    from_mate = swapped(to_mate, pair_mate)
    from_beside = swapped(to_other, beside_the_ends)
    high = call(last_kernel, (flags, other, own, high), [line], flops=tile)[0]
    beside_end = (me == 3) | (me == blocks - 4)
    returned = jnp.maximum(jnp.where(beside_end, LOWEST, from_first), from_mate)
    rest = jnp.where(beside_end, from_beside, LOWEST)
    return jnp.maximum(jnp.maximum(high, returned), rest).reshape(block)


def solution(mesh):
    in_specs = (P(AXES, None), P())
    out_specs = P(AXES)
    return jax.shard_map(shards, mesh=mesh, in_specs=in_specs, out_specs=out_specs, check_vma=False)
```
